32 devices in a mesh: group: 2 (over y), query: 8 (over z, x), row: 2 (over core).
Axes of the slice: x: 2, y: 2, z: 4, core: 2. Of those that a mesh axis runs over, the one named last changes fastest.
Arguments:
- query_left: bfloat16 [64, 32, 256], P(('group', 'query'), None, 'row'), parts along dimension 0, may hold values from -2.09375 to 2.09375
- query_right: bfloat16 [64, 32, 256], P(('group', 'query')), parts along dimension 0, may hold values from -2.09375 to 2.09375
- train_left: bfloat16 [64, 32, 256], P(('group', 'query'), None, 'row'), parts along dimension 0, may hold values from -2.09375 to 2.09375
- train_right: bfloat16 [64, 32, 256], P(('group', 'query')), parts along dimension 0, may hold values from -2.09375 to 2.09375
- eigenvalues: float32 [256, 256], P('row'), may hold values from 0.05 to 5
Outputs:
- influence: float32 [64, 32], P(('group', 'query')), parts along dimension 0
The draws below stay inside these ranges and needn't reach their ends.
There are 2 independent parts, one for each index of `group`. The reference program is written for one: setup_inputs(seed, part) draws one part's arguments, and reference() takes and returns one part's arrays. A program takes and returns all parts, laid end to end along the dimension named above; an argument that names none is the same for every part. Nothing has to cross between parts.
All inputs are finite; a program needn't handle non-finite values.
Results may differ from the reference program's by a relative error of at most 0.005.
Values may be sent and summed in bfloat16 or wider, within the bound.
A program may use at most 64 MiB of HBM per device.

```python
import math
import jax
import jax.numpy as jnp
from jax import lax

RANK = 32
ROWS = 256
COLS = 256
QUERIES = 32
TRAIN = 32


def level_of(stream_key, shape, split, low, high):
    gain = 1.0
    for position, parts in split:
        steps = jax.random.uniform(jax.random.fold_in(jax.random.fold_in(stream_key, 6), position), (parts,), jnp.float32, low / len(split), high / len(split))
        gain = gain * jnp.repeat(jnp.exp(steps), shape[position] // parts).reshape((-1,) + (1,) * (len(shape) - 1 - position))
    return gain


def scatter_about(own_key, dims, width, most, split=(), held_as=jnp.bfloat16):
    loudness = level_of(own_key, dims, split, -0.22, 0.18) if split else 1.0
    array = jax.random.normal(own_key, dims, jnp.float32) * width * loudness
    return jnp.minimum(jnp.maximum(array, -most), most).astype(held_as)


def setup_inputs(seed: int = 0, part: int = 0) -> dict:
    streams_of = jax.random.split(jax.random.key(seed), 6)
    part_keys = jax.random.split(jax.random.fold_in(streams_of[5], part), 6)
    query_left = scatter_about(part_keys[0], (QUERIES, RANK, ROWS), 0.35, 2.09375, ((0, 8), (2, 2)))
    query_right = scatter_about(part_keys[1], (QUERIES, RANK, COLS), 0.35, 2.09375, ((0, 8),))
    train_left = scatter_about(part_keys[2], (TRAIN, RANK, ROWS), 0.35, 2.09375, ((0, 8), (2, 2)))
    train_right = scatter_about(part_keys[3], (TRAIN, RANK, COLS), 0.35, 2.09375, ((0, 8),))
    eigenvalues = jnp.clip(jnp.exp(math.log(5.0) - 4.6051702 * jax.random.uniform(streams_of[4], (ROWS, COLS), jnp.float32) ** level_of(streams_of[4], (ROWS, COLS), ((0, 2),), -0.2, 0.2)), 0.05, 5.0)
    return dict(query_left=query_left, query_right=query_right, train_left=train_left, train_right=train_right, eigenvalues=eigenvalues)


damping = 0.05


def reference(query_left, query_right, train_left, train_right, eigenvalues):
    weight = 1.0 / (eigenvalues + damping)
    train_rows = train_left.astype(jnp.float32)
    train_cols = train_right.astype(jnp.float32)
    normalizer = float(ROWS * COLS) ** -0.5

    def per_query(operands):
        query_rows, query_cols = operands
        gradient = jnp.einsum("ra,rb->ab", query_rows.astype(jnp.float32), query_cols.astype(jnp.float32))
        rounded = (gradient * weight).astype(jnp.bfloat16)
        rounded = lax.optimization_barrier(rounded)
        precond = rounded.astype(jnp.float32)
        projected = jnp.einsum("ab,trb->tar", precond, train_cols)
        return jnp.einsum("tar,tra->t", projected, train_rows) * normalizer

    return lax.map(per_query, (query_left, query_right))
```

```python
import functools

import jax
import jax.numpy as jnp
from jax import lax
from jax.experimental import pallas as pl
from jax.experimental.pallas import tpu as pltpu
from jax.sharding import PartitionSpec as P

DAMPING = 0.05
MESH = pl.DeviceIdType.MESH


def each(count, step):
    if count <= 8:
        for k in range(count):
            step(k)
    else:
        lax.fori_loop(0, count, lambda k, _: (step(k), 0)[1], 0)


def kernel(
    halves,
    span,
    norm,
    ql_hbm,
    qr_hbm,
    tl_hbm,
    tr_hbm,
    eig_hbm,
    out_ref,
    ql,
    qr,
    tl,
    tr,
    eig,
    pre,
    acc,
    mine,
    parts,
    local_sem,
    q_send,
    q_recv,
    t_send,
    t_recv,
    r_send,
    r_recv,
):
    group = lax.axis_index("group")
    index = lax.axis_index("query")
    core = lax.axis_index("row")
    half = lax.div(index, span)
    place = lax.rem(index, span)
    count, rank, rows = ql_hbm.shape
    cols = qr_hbm.shape[2]

    def device(h, p, c):
        return (group, h * span + p, c)

    def place_of(d):
        return lax.bitwise_xor(place, d) if span & (span - 1) == 0 else lax.rem(place + d, span)

    def half_of(e):
        return lax.rem(half + e, halves)

    local = [
        pltpu.make_async_copy(eig_hbm, eig, local_sem.at[0]),
        pltpu.make_async_copy(ql_hbm, ql.at[half], local_sem.at[1]),
        pltpu.make_async_copy(qr_hbm, qr.at[half], local_sem.at[2]),
        pltpu.make_async_copy(tl_hbm, tl.at[place], local_sem.at[3]),
        pltpu.make_async_copy(tr_hbm, tr.at[place], local_sem.at[4]),
    ]
    for copy in local:
        copy.start()

    barrier = pltpu.get_barrier_semaphore()

    def greet(target):
        pl.semaphore_signal(barrier, inc=1, device_id=target, device_id_type=MESH)

    each(span - 1, lambda d: greet(device(half, place_of(d + 1), core)))
    for e in range(1, halves):
        for c in range(2):
            greet(device(half_of(e), place, c))
    greet(device(half, place, 1 - core))
    pl.semaphore_wait(barrier, span - 1 + 2 * (halves - 1) + 1)

    def q_copies(e, slot):
        target = device(half_of(e), place, core)
        return [
            pltpu.make_async_remote_copy(
                src, dst.at[slot], q_send.at[e, k], q_recv.at[slot, k],
                device_id=target, device_id_type=MESH,
            )
            for k, (src, dst) in enumerate([(ql_hbm, ql), (qr_hbm, qr)])
        ]

    def t_copies(d, slot):
        target = device(half, place_of(d), core)
        return [
            pltpu.make_async_remote_copy(
                src, dst.at[slot], t_send.at[d, k], t_recv.at[slot, k],
                device_id=target, device_id_type=MESH,
            )
            for k, (src, dst) in enumerate([(tr_hbm, tr), (tl_hbm, tl)])
        ]

    for e in range(1, halves):
        for copy in q_copies(e, half):
            copy.start()

    def send_t(d):
        for copy in t_copies(d + 1, place):
            copy.start()

    each(span - 1, send_t)

    local[0].wait()
    weight = jnp.transpose(1.0 / (eig[...] + DAMPING))
    local[1].wait()
    local[2].wait()

    def condition(h, position):
        for k in range(count):
            gradient = lax.dot_general(
                qr[h, k], ql[h, k], (((0,), (0,)), ((), ())), preferred_element_type=jnp.float32
            )
            start = (position * count + k) * rows
            pre[:, start : start + rows] = (gradient * weight).astype(jnp.bfloat16)

    condition(half, 0)
    for e in range(1, halves):
        slot = half_of(e)
        for copy in q_copies(e, slot):
            copy.wait_recv()
        condition(slot, e)
    local[3].wait()
    local[4].wait()
    queries = halves * count

    def score(d):
        slot = place_of(d)
        flat = tr[slot].reshape(count * rank, cols)
        left = tl[slot].astype(jnp.float32)
        for q in range(queries):
            projected = lax.dot_general(
                flat,
                pre[:, q * rows : (q + 1) * rows],
                (((1,), (0,)), ((), ())),
                preferred_element_type=jnp.float32,
            ).reshape(count, rank, rows)
            acc[slot, :, q, :] = jnp.sum(projected * left, axis=1)

    score(0)

    def score_next(d):
        for copy in t_copies(d + 1, place_of(d + 1)):
            copy.wait_recv()
        score(d + 1)

    each(span - 1, score_next)

    width = mine.shape[-1]
    lane = lax.broadcasted_iota(jnp.int32, (queries, width), 1)

    def gather(j, total):
        sums = jnp.sum(acc[j // count, j % count], axis=-1, keepdims=True)
        return jnp.where(lane == j, sums, total)

    total = jnp.zeros((queries, width), jnp.float32)
    pairs = span * count
    if pairs <= 32:
        for j in range(pairs):
            total = gather(j, total)
    else:
        total = lax.fori_loop(0, pairs, gather, total)
    total = total * norm
    for e in range(halves):
        mine[e] = total[e * count : (e + 1) * count]

    def r_copy(e, c, h, owner, k):
        return pltpu.make_async_remote_copy(
            mine.at[e], parts.at[h, owner], r_send.at[e, k], r_recv.at[h, owner],
            device_id=device(half_of(e), place, c), device_id_type=MESH,
        )

    results = []
    for e in range(1, halves):
        results.append(r_copy(e, core, half, core, 0))
        results.append(r_copy(e, 1 - core, half, core, 1))
    results.append(r_copy(0, 1 - core, half, core, 1))
    for copy in results:
        copy.start()
    parts[half, core] = mine[0]
    for e in range(1, halves):
        for c in range(2):
            r_copy(e, core, half_of(e), c, 0).wait_recv()
    r_copy(0, core, half, 1 - core, 0).wait_recv()
    out_ref[...] = jnp.concatenate(
        [(parts[h, 0] + parts[h, 1])[:, : span * count] for h in range(halves)], axis=1
    )
    for copy in results:
        copy.wait_send()
    for e in range(1, halves):
        for copy in q_copies(e, half):
            copy.wait_send()

    def sent_t(d):
        for copy in t_copies(d + 1, place):
            copy.wait_send()

    each(span - 1, sent_t)


def solution(mesh):
    n = mesh.shape["query"]
    halves = 2 if n % 2 == 0 else 1
    span = n // halves

    def body(query_left, query_right, train_left, train_right, eigenvalues):
        count, rank, rows = query_left.shape
        cols = query_right.shape[2]
        norm = float(rows * mesh.shape["row"] * cols) ** -0.5
        width = -(-span * count // 128) * 128
        bf16, f32 = jnp.bfloat16, jnp.float32
        return pl.pallas_call(
            functools.partial(kernel, halves, span, norm),
            out_shape=jax.ShapeDtypeStruct((count, n * count), f32),
            in_specs=[pl.BlockSpec(memory_space=pl.ANY)] * 5,
            out_specs=pl.BlockSpec(memory_space=pltpu.VMEM),
            scratch_shapes=[
                pltpu.VMEM((halves, count, rank, rows), bf16),
                pltpu.VMEM((halves, count, rank, cols), bf16),
                pltpu.VMEM((span, count, rank, rows), bf16),
                pltpu.VMEM((span, count, rank, cols), bf16),
                pltpu.VMEM((rows, cols), f32),
                pltpu.VMEM((cols, halves * count * rows), bf16),
                pltpu.VMEM((span, count, halves * count, rows), f32),
                pltpu.VMEM((halves, count, width), f32),
                pltpu.VMEM((halves, 2, count, width), f32),
                pltpu.SemaphoreType.DMA((5,)),
                pltpu.SemaphoreType.DMA((halves, 2)),
                pltpu.SemaphoreType.DMA((halves, 2)),
                pltpu.SemaphoreType.DMA((span, 2)),
                pltpu.SemaphoreType.DMA((span, 2)),
                pltpu.SemaphoreType.DMA((halves, 2)),
                pltpu.SemaphoreType.DMA((halves, 2)),
            ],
            compiler_params=pltpu.CompilerParams(
                collective_id=0, has_side_effects=True, vmem_limit_bytes=32 * 1024 * 1024
            ),
        )(query_left, query_right, train_left, train_right, eigenvalues)

    placed = (
        P(("group", "query"), None, "row"),
        P(("group", "query"), None, None),
        P(("group", "query"), None, "row"),
        P(("group", "query"), None, None),
        P("row", None),
    )
    return jax.shard_map(
        body, mesh=mesh, in_specs=placed, out_specs=P(("group", "query"), None), check_vma=False
    )
```

```python
import functools

import jax
import jax.numpy as jnp
from jax import lax
from jax.experimental import pallas as pl
from jax.experimental.pallas import tpu as pltpu
from jax.sharding import PartitionSpec as P

DAMPING = 0.05
MESH = pl.DeviceIdType.MESH


def each(count, step):
    if count <= 8:
        for k in range(count):
            step(k)
    else:
        lax.fori_loop(0, count, lambda k, _: (step(k), 0)[1], 0)


def kernel(
    halves,
    span,
    norm,
    ql_hbm,
    qr_hbm,
    tl_hbm,
    tr_hbm,
    eig_hbm,
    out_ref,
    ql,
    qr,
    tl,
    tr,
    eig,
    pre,
    acc,
    mine,
    parts,
    local_sem,
    q_send,
    q_recv,
    t_send,
    t_recv,
    r_send,
    r_recv,
):
    group = lax.axis_index("group")
    index = lax.axis_index("query")
    core = lax.axis_index("row")
    half = lax.div(index, span)
    place = lax.rem(index, span)
    count, rank, rows = ql_hbm.shape
    cols = qr_hbm.shape[2]

    def device(h, p, c):
        return (group, h * span + p, c)

    def place_of(d):
        return lax.bitwise_xor(place, d) if span & (span - 1) == 0 else lax.rem(place + d, span)

    def half_of(e):
        return lax.rem(half + e, halves)

    local = [
        pltpu.make_async_copy(eig_hbm, eig, local_sem.at[0]),
        pltpu.make_async_copy(ql_hbm, ql.at[half], local_sem.at[1]),
        pltpu.make_async_copy(qr_hbm, qr.at[half], local_sem.at[2]),
        pltpu.make_async_copy(tl_hbm, tl.at[place], local_sem.at[3]),
        pltpu.make_async_copy(tr_hbm, tr.at[place], local_sem.at[4]),
    ]
    for copy in local:
        copy.start()

    barrier = pltpu.get_barrier_semaphore()

    def greet(target):
        pl.semaphore_signal(barrier, inc=1, device_id=target, device_id_type=MESH)

    each(span - 1, lambda d: greet(device(half, place_of(d + 1), core)))
    for e in range(1, halves):
        for c in range(2):
            greet(device(half_of(e), place, c))
    greet(device(half, place, 1 - core))
    pl.semaphore_wait(barrier, span - 1 + 2 * (halves - 1) + 1)

    def q_copies(e, slot):
        target = device(half_of(e), place, core)
        return [
            pltpu.make_async_remote_copy(
                src, dst.at[slot], q_send.at[e, k], q_recv.at[slot, k],
                device_id=target, device_id_type=MESH,
            )
            for k, (src, dst) in enumerate([(ql_hbm, ql), (qr_hbm, qr)])
        ]

    def t_copies(d, slot):
        target = device(half, place_of(d), core)
        return [
            pltpu.make_async_remote_copy(
                src, dst.at[slot], t_send.at[d, k], t_recv.at[slot, k],
                device_id=target, device_id_type=MESH,
            )
            for k, (src, dst) in enumerate([(tr_hbm, tr), (tl_hbm, tl)])
        ]

    for e in range(1, halves):
        for copy in q_copies(e, half):
            copy.start()

    def send_t(d):
        for copy in t_copies(d + 1, place):
            copy.start()

    each(span - 1, send_t)

    local[0].wait()
    weight = jnp.transpose(1.0 / (eig[...] + DAMPING))
    local[1].wait()
    local[2].wait()

    def condition(h, position):
        for k in range(count):
            gradient = lax.dot_general(
                qr[h, k], ql[h, k], (((0,), (0,)), ((), ())), preferred_element_type=jnp.float32
            )
            start = (position * count + k) * rows
            pre[:, start : start + rows] = (gradient * weight).astype(jnp.bfloat16)

    condition(half, 0)
    for e in range(1, halves):
        slot = half_of(e)
        for copy in q_copies(e, slot):
            copy.wait_recv()
        condition(slot, e)
    local[3].wait()
    local[4].wait()
    queries = halves * count

    def score(d):
        slot = place_of(d)
        flat = tr[slot].reshape(count * rank, cols)
        left = tl[slot].astype(jnp.float32)
        for q in range(queries):
            projected = lax.dot_general(
                flat,
                pre[:, q * rows : (q + 1) * rows],
                (((1,), (0,)), ((), ())),
                preferred_element_type=jnp.float32,
            ).reshape(count, rank, rows)
            acc[slot, :, q, :] = jnp.sum(projected * left, axis=1)

    score(0)

    def score_next(d):
        for copy in t_copies(d + 1, place_of(d + 1)):
            copy.wait_recv()
        score(d + 1)

    each(span - 1, score_next)

    width = mine.shape[-1]
    lane = lax.broadcasted_iota(jnp.int32, (queries, width), 1)

    def gather(j, total):
        sums = jnp.sum(acc[j // count, j % count], axis=-1, keepdims=True)
        return jnp.where(lane == j, sums, total)

    total = jnp.zeros((queries, width), jnp.float32)
    pairs = span * count
    if pairs <= 32:
        for j in range(pairs):
            total = gather(j, total)
    else:
        total = lax.fori_loop(0, pairs, gather, total)
    total = total * norm
    for e in range(halves):
        mine[e] = total[e * count : (e + 1) * count]

    def r_copy(e, c, h, owner, k):
        return pltpu.make_async_remote_copy(
            mine.at[e], parts.at[h, owner], r_send.at[e, k], r_recv.at[h, owner],
            device_id=device(half_of(e), place, c), device_id_type=MESH,
        )

    results = []
    for e in range(1, halves):
        results.append(r_copy(e, core, half, core, 0))
        results.append(r_copy(e, 1 - core, half, core, 1))
    results.append(r_copy(0, 1 - core, half, core, 1))
    for copy in results:
        copy.start()
    parts[half, core] = mine[0]
    for e in range(1, halves):
        for c in range(2):
            r_copy(e, core, half_of(e), c, 0).wait_recv()
    r_copy(0, core, half, 1 - core, 0).wait_recv()
    out_ref[...] = jnp.concatenate(
        [(parts[h, 0] + parts[h, 1])[:, : span * count] for h in range(halves)], axis=1
    )
    for copy in results:
        copy.wait_send()
    for e in range(1, halves):
        for copy in q_copies(e, half):
            copy.wait_send()

    def sent_t(d):
        for copy in t_copies(d + 1, place):
            copy.wait_send()

    each(span - 1, sent_t)


def solution(mesh):
    n = mesh.shape["query"]
    halves = 2 if n % 2 == 0 else 1
    span = n // halves

    def body(query_left, query_right, train_left, train_right, eigenvalues):
        count, rank, rows = query_left.shape
        cols = query_right.shape[2]
        norm = float(rows * mesh.shape["row"] * cols) ** -0.5
        width = -(-span * count // 128) * 128
        bf16, f32 = jnp.bfloat16, jnp.float32
        return pl.pallas_call(
            functools.partial(kernel, halves, span, norm),
            out_shape=jax.ShapeDtypeStruct((count, n * count), f32),
            in_specs=[pl.BlockSpec(memory_space=pl.ANY)] * 5,
            out_specs=pl.BlockSpec(memory_space=pltpu.VMEM),
            scratch_shapes=[
                pltpu.VMEM((halves, count, rank, rows), bf16),
                pltpu.VMEM((halves, count, rank, cols), bf16),
                pltpu.VMEM((span, count, rank, rows), bf16),
                pltpu.VMEM((span, count, rank, cols), bf16),
                pltpu.VMEM((rows, cols), f32),
                pltpu.VMEM((cols, halves * count * rows), bf16),
                pltpu.VMEM((span, count, halves * count, rows), f32),
                pltpu.VMEM((halves, count, width), f32),
                pltpu.VMEM((halves, 2, count, width), f32),
                pltpu.SemaphoreType.DMA((5,)),
                pltpu.SemaphoreType.DMA((halves, 2)),
                pltpu.SemaphoreType.DMA((halves, 2)),
                pltpu.SemaphoreType.DMA((span, 2)),
                pltpu.SemaphoreType.DMA((span, 2)),
                pltpu.SemaphoreType.DMA((halves, 2)),
                pltpu.SemaphoreType.DMA((halves, 2)),
            ],
            compiler_params=pltpu.CompilerParams(
                collective_id=0, has_side_effects=True, vmem_limit_bytes=60 * 1024 * 1024
            ),
        )(query_left, query_right, train_left, train_right, eigenvalues)

    placed = (
        P(("group", "query"), None, "row"),
        P(("group", "query"), None, None),
        P(("group", "query"), None, "row"),
        P(("group", "query"), None, None),
        P("row", None),
    )
    return jax.shard_map(
        body, mesh=mesh, in_specs=placed, out_specs=P(("group", "query"), None), check_vma=False
    )
```

```python
import functools

import jax
import jax.numpy as jnp
from jax import lax
from jax.experimental import pallas as pl
from jax.experimental.pallas import tpu as pltpu
from jax.sharding import PartitionSpec as P

DAMPING = 0.05
MESH = pl.DeviceIdType.MESH


def each(count, step, carry):
    if count <= 8:
        for k in range(count):
            carry = step(k, carry)
        return carry
    return lax.fori_loop(0, count, step, carry)


def kernel(
    halves,
    span,
    norm,
    ql_hbm,
    qr_hbm,
    tl_hbm,
    tr_hbm,
    eig_hbm,
    out_ref,
    ql,
    qr,
    tl,
    tr,
    eig,
    pre,
    acc,
    mine,
    parts,
    local_sem,
    s_send,
    s_recv,
    q_send,
    q_recv,
    f_send,
    f_recv,
    t_send,
    t_recv,
    r_send,
    r_recv,
):
    group = lax.axis_index("group")
    index = lax.axis_index("query")
    core = lax.axis_index("row")
    other = 1 - core
    half = lax.div(index, span)
    place = lax.rem(index, span)
    count, rank, rows = ql_hbm.shape
    cols = qr_hbm.shape[2]
    share = count // 2
    here, there = pl.ds(core * share, share), pl.ds(other * share, share)

    def place_of(d):
        return lax.bitwise_xor(place, d) if span & (span - 1) == 0 else lax.rem(place + d, span)

    def half_of(e):
        return lax.rem(half + e, halves)

    local = [
        pltpu.make_async_copy(src, dst, local_sem.at[k])
        for k, (src, dst) in enumerate(
            [
                (eig_hbm, eig.at[core]),
                (ql_hbm, ql.at[half, core]),
                (qr_hbm, qr.at[half]),
                (tl_hbm.at[here], tl.at[place, core]),
                (tr_hbm.at[here], tr.at[place]),
            ]
        )
    ]
    for copy in local:
        copy.start()

    barrier = pltpu.get_barrier_semaphore()

    def greet(h, p, c):
        pl.semaphore_signal(barrier, inc=1, device_id=(group, h * span + p, c), device_id_type=MESH)

    def greet_span(d, carry):
        greet(half, place_of(d + 1), core)
        greet(half, place_of(d + 1), other)
        return carry

    each(span - 1, greet_span, 0)
    for e in range(1, halves):
        greet(half_of(e), place, core)
        greet(half_of(e), place, other)
    greet(half, place, other)
    pl.semaphore_wait(barrier, 2 * (span - 1) + 2 * (halves - 1) + 1)

    def remote(src, dst, send, recv, h, p, c):
        return pltpu.make_async_remote_copy(
            src, dst, send, recv, device_id=(group, h * span + p, c), device_id_type=MESH
        )

    def s_copies(a):
        pairs = [
            (eig_hbm, eig.at[a]),
            (ql_hbm, ql.at[half, a]),
            (tl_hbm.at[there], tl.at[place, a]),
        ]
        return [
            remote(src, dst, s_send.at[k], s_recv.at[k], half, place, other)
            for k, (src, dst) in enumerate(pairs)
        ]

    def q_copies(e, h):
        pairs = [
            (ql_hbm, ql.at[h, core]),
            (qr_hbm.at[here], qr.at[h, here]),
        ]
        return [
            remote(src, dst, q_send.at[e, k], q_recv.at[h, k], half_of(e), place, core)
            for k, (src, dst) in enumerate(pairs)
        ]

    def f_copies(h, a, part):
        refs = [ql.at[h, a], qr.at[h, part]]
        return [
            remote(ref, ref, f_send.at[h, k], f_recv.at[h, k], half, place, other)
            for k, ref in enumerate(refs)
        ]

    def t_copies(d, p, a, b):
        target = place_of(d)
        triples = [
            (tr_hbm.at[here], tr.at[p], core),
            (tl_hbm.at[here], tl.at[p, a], core),
            (tl_hbm.at[there], tl.at[p, b], other),
        ]
        return [
            remote(src, dst, t_send.at[d, k], t_recv.at[p, k], half, target, c)
            for k, (src, dst, c) in enumerate(triples)
        ]

    for e in range(1, halves):
        for copy in q_copies(e, half):
            copy.start()
    for copy in s_copies(core):
        copy.start()

    def send_t(d, carry):
        for copy in t_copies(span - 1 - d, place, core, core):
            copy.start()
        return carry

    each(span - 1, send_t, 0)

    local[0].wait()
    local[1].wait()
    local[2].wait()
    arrivals = s_copies(other)
    arrivals[0].wait_recv()
    weight = jnp.concatenate(
        [jnp.transpose(1.0 / (eig[a] + DAMPING)) for a in range(2)], axis=1
    )
    arrivals[1].wait_recv()

    def condition(h, e):
        for k in range(count):
            gradient = lax.dot_general(
                qr[h, k],
                jnp.concatenate([ql[h, 0, k], ql[h, 1, k]], axis=1),
                (((0,), (0,)), ((), ())),
                preferred_element_type=jnp.float32,
            )
            start = (e * count + k) * 2 * rows
            pre[:, start : start + 2 * rows] = (gradient * weight).astype(jnp.bfloat16)

    width = mine.shape[-1]
    lane = lax.broadcasted_iota(jnp.int32, (count, width), 1)

    def score(d, e, total):
        slot = place_of(d)
        flat = tr[slot].reshape(share * rank, cols)
        left = [tl[slot, a].astype(jnp.float32) for a in range(2)]
        for k in range(count):
            start = (e * count + k) * 2 * rows
            projected = lax.dot_general(
                flat,
                pre[:, start : start + 2 * rows],
                (((1,), (0,)), ((), ())),
                preferred_element_type=jnp.float32,
            )
            product = (
                projected[:, :rows].reshape(share, rank, rows) * left[0]
                + projected[:, rows:].reshape(share, rank, rows) * left[1]
            )
            acc[e, :, k, :] = jnp.sum(product, axis=1)
        for t in range(share):
            sums = jnp.sum(acc[e, t], axis=-1, keepdims=True)
            total = jnp.where(lane == slot * count + core * share + t, sums, total)
        return total

    totals = [jnp.zeros((count, width), jnp.float32)] * halves
    condition(half, 0)
    local[3].wait()
    local[4].wait()
    arrivals[2].wait_recv()
    totals[0] = score(0, 0, totals[0])
    for e in range(1, halves):
        for copy in q_copies(e, half_of(e)):
            copy.wait_recv()
        for copy in f_copies(half_of(e), core, here):
            copy.start()
    for e in range(1, halves):
        for copy in f_copies(half_of(e), other, there):
            copy.wait_recv()
        condition(half_of(e), e)
        totals[e] = score(0, e, totals[e])

    def arrive(d):
        for copy in t_copies(d, place_of(d), core, other):
            copy.wait_recv()

    def score_next(d, totals):
        arrive(d + 1)
        return [score(d + 1, e, totals[e]) for e in range(halves)]

    totals = each(span - 2, score_next, totals)

    def r_copy(e, c, h, owner, k):
        return remote(mine.at[e], parts.at[h, owner], r_send.at[e, k], r_recv.at[h, owner], half_of(e), place, c)

    arrive(span - 1)
    results = []
    for e in [*range(1, halves), 0]:
        mine[e] = score(span - 1, e, totals[e]) * norm
        copies = [r_copy(e, other, half, core, 1)]
        if e:
            copies.append(r_copy(e, core, half, core, 0))
        for copy in copies:
            copy.start()
        results += copies
    parts[half, core] = mine[0]
    r_copy(0, core, half, other, 0).wait_recv()
    for e in range(1, halves):
        for c in range(2):
            r_copy(e, core, half_of(e), c, 0).wait_recv()
    out_ref[...] = jnp.concatenate(
        [(parts[h, 0] + parts[h, 1])[:, : span * count] for h in range(halves)], axis=1
    )
    for copy in results:
        copy.wait_send()
    for copy in s_copies(core):
        copy.wait_send()
    for e in range(1, halves):
        for copy in q_copies(e, half):
            copy.wait_send()
        for copy in f_copies(half_of(e), core, here):
            copy.wait_send()

    def sent_t(d, carry):
        for copy in t_copies(d + 1, place, core, core):
            copy.wait_send()
        return carry

    each(span - 1, sent_t, 0)


def solution(mesh):
    n = mesh.shape["query"]
    halves = 2 if n % 2 == 0 else 1
    span = n // halves

    def body(*operands):
        count, rank, rows = operands[0].shape
        cols = operands[1].shape[2]
        norm = float(rows * mesh.shape["row"] * cols) ** -0.5
        width = -(-span * count // 128) * 128
        bf16, f32 = jnp.bfloat16, jnp.float32
        return pl.pallas_call(
            functools.partial(kernel, halves, span, norm),
            out_shape=jax.ShapeDtypeStruct((count, n * count), f32),
            in_specs=[pl.BlockSpec(memory_space=pl.ANY)] * 5,
            out_specs=pl.BlockSpec(memory_space=pltpu.VMEM),
            scratch_shapes=[
                pltpu.VMEM((halves, 2, count, rank, rows), bf16),
                pltpu.VMEM((halves, count, rank, cols), bf16),
                pltpu.VMEM((span, 2, count // 2, rank, rows), bf16),
                pltpu.VMEM((span, count // 2, rank, cols), bf16),
                pltpu.VMEM((2, rows, cols), f32),
                pltpu.VMEM((cols, halves * count * 2 * rows), bf16),
                pltpu.VMEM((halves, count // 2, count, rows), f32),
                pltpu.VMEM((halves, count, width), f32),
                pltpu.VMEM((halves, 2, count, width), f32),
                pltpu.SemaphoreType.DMA((5,)),
                pltpu.SemaphoreType.DMA((3,)),
                pltpu.SemaphoreType.DMA((3,)),
                pltpu.SemaphoreType.DMA((halves, 2)),
                pltpu.SemaphoreType.DMA((halves, 2)),
                pltpu.SemaphoreType.DMA((halves, 2)),
                pltpu.SemaphoreType.DMA((halves, 2)),
                pltpu.SemaphoreType.DMA((span, 3)),
                pltpu.SemaphoreType.DMA((span, 3)),
                pltpu.SemaphoreType.DMA((halves, 2)),
                pltpu.SemaphoreType.DMA((halves, 2)),
            ],
            compiler_params=pltpu.CompilerParams(
                collective_id=0, has_side_effects=True, vmem_limit_bytes=32 * 1024 * 1024
            ),
        )(*(pltpu.with_memory_space_constraint(x, pltpu.HBM) for x in operands))

    placed = (
        P(("group", "query"), None, "row"),
        P(("group", "query"), None, None),
        P(("group", "query"), None, "row"),
        P(("group", "query"), None, None),
        P("row", None),
    )
    return jax.shard_map(
        body, mesh=mesh, in_specs=placed, out_specs=P(("group", "query"), None), check_vma=False
    )
```

```python
import functools

import jax
import jax.numpy as jnp
from jax import lax
from jax.experimental import pallas as pl
from jax.experimental.pallas import tpu as pltpu
from jax.sharding import PartitionSpec as P

DAMPING = 0.05
MESH = pl.DeviceIdType.MESH


def each(count, step, carry):
    if count <= 8:
        for k in range(count):
            carry = step(k, carry)
        return carry
    return lax.fori_loop(0, count, step, carry)


def kernel(
    halves,
    span,
    norm,
    ql_hbm,
    qr_hbm,
    tl_hbm,
    tr_hbm,
    eig_hbm,
    out_ref,
    ql,
    qr,
    tl,
    tr,
    eig,
    pre,
    acc,
    mine,
    parts,
    local_sem,
    s_send,
    s_recv,
    q_send,
    q_recv,
    f_send,
    f_recv,
    t_send,
    t_recv,
    r_send,
    r_recv,
):
    group = lax.axis_index("group")
    index = lax.axis_index("query")
    core = lax.axis_index("row")
    other = 1 - core
    half = lax.div(index, span)
    place = lax.rem(index, span)
    count, rank, rows = ql_hbm.shape
    cols = qr_hbm.shape[2]
    share = count // 2
    here, there = pl.ds(core * share, share), pl.ds(other * share, share)

    def place_of(d):
        return lax.bitwise_xor(place, d) if span & (span - 1) == 0 else lax.rem(place + d, span)

    def half_of(e):
        return lax.rem(half + e, halves)

    local = [
        pltpu.make_async_copy(src, dst, local_sem.at[k])
        for k, (src, dst) in enumerate(
            [
                (eig_hbm, eig.at[core]),
                (ql_hbm, ql.at[half, core]),
                (qr_hbm, qr.at[half]),
                (tl_hbm.at[here], tl.at[place, core]),
                (tr_hbm.at[here], tr.at[place]),
            ]
        )
    ]
    for copy in local:
        copy.start()

    barrier = pltpu.get_barrier_semaphore()

    def greet(h, p, c):
        pl.semaphore_signal(barrier, inc=1, device_id=(group, h * span + p, c), device_id_type=MESH)

    def greet_span(d, carry):
        greet(half, place_of(d + 1), core)
        greet(half, place_of(d + 1), other)
        return carry

    each(span - 1, greet_span, 0)
    for e in range(1, halves):
        greet(half_of(e), place, core)
        greet(half_of(e), place, other)
    greet(half, place, other)
    pl.semaphore_wait(barrier, 2 * (span - 1) + 2 * (halves - 1) + 1)

    def remote(src, dst, send, recv, h, p, c):
        return pltpu.make_async_remote_copy(
            src, dst, send, recv, device_id=(group, h * span + p, c), device_id_type=MESH
        )

    def s_copies(a):
        pairs = [
            (eig_hbm, eig.at[a]),
            (ql_hbm, ql.at[half, a]),
            (tl_hbm.at[there], tl.at[place, a]),
        ]
        return [
            remote(src, dst, s_send.at[k], s_recv.at[k], half, place, other)
            for k, (src, dst) in enumerate(pairs)
        ]

    def q_copies(e, h):
        pairs = [
            (ql_hbm, ql.at[h, core]),
            (qr_hbm.at[here], qr.at[h, here]),
        ]
        return [
            remote(src, dst, q_send.at[e, k], q_recv.at[h, k], half_of(e), place, core)
            for k, (src, dst) in enumerate(pairs)
        ]

    def f_copies(h, a, part):
        refs = [ql.at[h, a], qr.at[h, part]]
        return [
            remote(ref, ref, f_send.at[h, k], f_recv.at[h, k], half, place, other)
            for k, ref in enumerate(refs)
        ]

    def t_copies(d, p, a, b):
        target = place_of(d)
        triples = [
            (tr_hbm.at[here], tr.at[p], core),
            (tl_hbm.at[here], tl.at[p, a], core),
            (tl_hbm.at[there], tl.at[p, b], other),
        ]
        return [
            remote(src, dst, t_send.at[d, k], t_recv.at[p, k], half, target, c)
            for k, (src, dst, c) in enumerate(triples)
        ]

    for e in range(1, halves):
        for copy in q_copies(e, half):
            copy.start()
    for copy in s_copies(core):
        copy.start()

    def send_t(d, carry):
        for copy in t_copies(span - 1 - d, place, core, core):
            copy.start()
        return carry

    each(span - 1, send_t, 0)

    local[0].wait()
    local[1].wait()
    local[2].wait()
    arrivals = s_copies(other)
    arrivals[0].wait_recv()
    weight = jnp.concatenate(
        [jnp.transpose(1.0 / (eig[a] + DAMPING)) for a in range(2)], axis=1
    )
    arrivals[1].wait_recv()

    def condition(h, e):
        for k in range(count):
            gradient = lax.dot_general(
                qr[h, k],
                jnp.concatenate([ql[h, 0, k], ql[h, 1, k]], axis=1),
                (((0,), (0,)), ((), ())),
                preferred_element_type=jnp.float32,
            )
            start = (e * count + k) * 2 * rows
            pre[:, start : start + 2 * rows] = (gradient * weight).astype(jnp.bfloat16)

    width = mine.shape[-1]
    lane = lax.broadcasted_iota(jnp.int32, (count, width), 1)

    def score(d, e, total):
        slot = place_of(d)
        flat = tr[slot].reshape(share * rank, cols)
        left = [tl[slot, a].astype(jnp.float32) for a in range(2)]
        for k in range(count):
            start = (e * count + k) * 2 * rows
            projected = lax.dot_general(
                flat,
                pre[:, start : start + 2 * rows],
                (((1,), (0,)), ((), ())),
                preferred_element_type=jnp.float32,
            )
            product = (
                projected[:, :rows].reshape(share, rank, rows) * left[0]
                + projected[:, rows:].reshape(share, rank, rows) * left[1]
            )
            acc[e, :, k, :] = jnp.sum(product, axis=1)
        for t in range(share):
            sums = jnp.sum(acc[e, t], axis=-1, keepdims=True)
            total = jnp.where(lane == slot * count + core * share + t, sums, total)
        return total

    totals = [jnp.zeros((count, width), jnp.float32)] * halves
    condition(half, 0)
    local[3].wait()
    local[4].wait()
    arrivals[2].wait_recv()
    totals[0] = score(0, 0, totals[0])
    for e in range(1, halves):
        for copy in q_copies(e, half_of(e)):
            copy.wait_recv()
        for copy in f_copies(half_of(e), core, here):
            copy.start()

    def r_copy(e, c, h, owner, k):
        return remote(mine.at[e], parts.at[h, owner], r_send.at[e, k], r_recv.at[h, owner], half_of(e), place, c)

    def score_own(d, total):
        for copy in t_copies(d + 1, place_of(d + 1), core, other):
            copy.wait_recv()
        return score(d + 1, 0, total)

    mine[0] = each(span - 1, score_own, totals[0]) * norm
    results = [r_copy(0, other, half, core, 1)]
    results[0].start()
    for e in range(1, halves):
        for copy in f_copies(half_of(e), other, there):
            copy.wait_recv()
        condition(half_of(e), e)
        mine[e] = each(span, lambda d, total: score(d, e, total), totals[e]) * norm
        copies = [r_copy(e, other, half, core, 1), r_copy(e, core, half, core, 0)]
        for copy in copies:
            copy.start()
        results += copies
    parts[half, core] = mine[0]
    r_copy(0, core, half, other, 0).wait_recv()
    for e in range(1, halves):
        for c in range(2):
            r_copy(e, core, half_of(e), c, 0).wait_recv()
    out_ref[...] = jnp.concatenate(
        [(parts[h, 0] + parts[h, 1])[:, : span * count] for h in range(halves)], axis=1
    )
    for copy in results:
        copy.wait_send()
    for copy in s_copies(core):
        copy.wait_send()
    for e in range(1, halves):
        for copy in q_copies(e, half):
            copy.wait_send()
        for copy in f_copies(half_of(e), core, here):
            copy.wait_send()

    def sent_t(d, carry):
        for copy in t_copies(d + 1, place, core, core):
            copy.wait_send()
        return carry

    each(span - 1, sent_t, 0)


def solution(mesh):
    n = mesh.shape["query"]
    halves = 2 if n % 2 == 0 else 1
    span = n // halves

    def body(*operands):
        count, rank, rows = operands[0].shape
        cols = operands[1].shape[2]
        norm = float(rows * mesh.shape["row"] * cols) ** -0.5
        width = -(-span * count // 128) * 128
        bf16, f32 = jnp.bfloat16, jnp.float32
        return pl.pallas_call(
            functools.partial(kernel, halves, span, norm),
            out_shape=jax.ShapeDtypeStruct((count, n * count), f32),
            in_specs=[pl.BlockSpec(memory_space=pl.ANY)] * 5,
            out_specs=pl.BlockSpec(memory_space=pltpu.VMEM),
            scratch_shapes=[
                pltpu.VMEM((halves, 2, count, rank, rows), bf16),
                pltpu.VMEM((halves, count, rank, cols), bf16),
                pltpu.VMEM((span, 2, count // 2, rank, rows), bf16),
                pltpu.VMEM((span, count // 2, rank, cols), bf16),
                pltpu.VMEM((2, rows, cols), f32),
                pltpu.VMEM((cols, halves * count * 2 * rows), bf16),
                pltpu.VMEM((halves, count // 2, count, rows), f32),
                pltpu.VMEM((halves, count, width), f32),
                pltpu.VMEM((halves, 2, count, width), f32),
                pltpu.SemaphoreType.DMA((5,)),
                pltpu.SemaphoreType.DMA((3,)),
                pltpu.SemaphoreType.DMA((3,)),
                pltpu.SemaphoreType.DMA((halves, 2)),
                pltpu.SemaphoreType.DMA((halves, 2)),
                pltpu.SemaphoreType.DMA((halves, 2)),
                pltpu.SemaphoreType.DMA((halves, 2)),
                pltpu.SemaphoreType.DMA((span, 3)),
                pltpu.SemaphoreType.DMA((span, 3)),
                pltpu.SemaphoreType.DMA((halves, 2)),
                pltpu.SemaphoreType.DMA((halves, 2)),
            ],
            compiler_params=pltpu.CompilerParams(
                collective_id=0, has_side_effects=True, vmem_limit_bytes=32 * 1024 * 1024
            ),
        )(*(pltpu.with_memory_space_constraint(x, pltpu.HBM) for x in operands))

    placed = (
        P(("group", "query"), None, "row"),
        P(("group", "query"), None, None),
        P(("group", "query"), None, "row"),
        P(("group", "query"), None, None),
        P("row", None),
    )
    return jax.shard_map(
        body, mesh=mesh, in_specs=placed, out_specs=P(("group", "query"), None), check_vma=False
    )
```
